256 devices in a mesh: batch: 64 (over y, z_lo, x), rep: 4 (over z_hi, core).
Axes of the slice: x: 4, y: 4, z: 8 (z_hi: 2, z_lo: 4; z = z_hi * 4 + z_lo), core: 2. Of those that a mesh axis runs over, the one named last changes fastest.
Arguments:
- images: bfloat16 [65536, 1152], P(('batch', 'rep')), may hold values from -0.41015625 to 0.41015625
- caption_vectors: bfloat16 [65536, 1152], P(('batch', 'rep')), may hold values from -0.41015625 to 0.41015625
- sample_weight: float32 [65536], P(('batch', 'rep')), may hold values from 0.4 to 22.5, as said below
- natural_odds_factor: float32 [1], replicated, may hold values from 1.6 to 2.8
- bias: float32 [1], replicated, may hold values from -3 to -1
Outputs:
- loss: float32 [1], replicated
- grad_scalars: float32 [2], replicated
- grad_images: bfloat16 [65536, 1152], P(('batch', 'rep'))
- grad_texts: bfloat16 [65536, 1152], P(('batch', 'rep'))
The draws below stay inside these ranges and needn't reach their ends.
Inputs may be any that keep to these rules, and one draw needn't show every extreme that they name: `sample_weight`: positive weights.
All inputs are finite; a program needn't handle non-finite values.
Results may differ from the reference program's by a relative error of at most 0.017.
Values may be sent and summed in bfloat16 or wider, within the bound.
No kernel may reach another device: no remote copies, remote signals or barrier semaphores. Data moves between devices by JAX's collectives and lax.ppermute only.
A program may use at most 128 MiB of HBM per device.

```python
import jax
import jax.numpy as jnp
import numpy as np
from jax import lax

D = 1152
ROUNDS = 3
GROUPS = 64
ROWS = 1024
TOKENS = 65536


def draw_sample_weight(key, part):
    key = jax.random.fold_in(key, 7)
    position = jnp.arange(TOKENS, dtype=jnp.float32) / TOKENS
    trend = jnp.exp(position * jnp.log(3.0))
    noise = jnp.exp(jax.random.uniform(key, (TOKENS,), jnp.float32, jnp.log(0.5), jnp.log(2.0)))
    return (trend * noise).astype(jnp.float32)


def steps_of(stream_key, extent, split, smallest, largest):
    factor_of, own = 1.0, jax.random.fold_in(stream_key, 6)
    for dim, parts in split:
        heights = jnp.exp(jax.random.uniform(jax.random.fold_in(own, dim), (parts,), jnp.float32, smallest / len(split), largest / len(split)))
        factor_of = factor_of * jnp.repeat(heights, extent[dim] // parts).reshape([-1 if axis == dim else 1 for axis in range(len(extent))])
    return factor_of


def scatter_about(stream_key, extent, scale, reach, cuts=(), kind=jnp.bfloat16):
    values = scale * jax.random.normal(stream_key, extent, jnp.float32)
    if cuts:
        values = values * steps_of(stream_key, extent, cuts, -0.22, 0.18)
    return jnp.clip(values, -reach, reach).astype(kind)


def setup_inputs(seed: int = 0) -> dict:
    key_of = jax.random.split(jax.random.key(seed), 6)
    return {
        "images": scatter_about(key_of[0], (TOKENS, D), (0.4 * D ** -0.25), 0.41015625, ((0, 256),)),
        "caption_vectors": scatter_about(key_of[1], (TOKENS, D), (0.4 * D ** -0.25), 0.41015625, ((0, 256),)),
        "sample_weight": draw_sample_weight(jax.random.fold_in(key_of[5], 71), 0),
        "natural_odds_factor": jnp.clip(jax.random.uniform(key_of[3], (1,), jnp.float32, 1.6, 2.8), 1.6, 2.8),
        "bias": jnp.clip(jax.random.uniform(key_of[4], (1,), jnp.float32, -3.0, -1.0), -3.0, -1.0),
    }


def companion_tile(picture_line_group, caption_line_group, example_importance, odds_sharpness, line_start_shift, matching_indicator):
    couple_similarity = jnp.dot(picture_line_group, caption_line_group.T, preferred_element_type=jnp.float32)
    couple_odds = odds_sharpness * couple_similarity + line_start_shift
    importance_similarity = example_importance[:, None] * (jax.nn.sigmoid(couple_odds) - matching_indicator)
    couple_strength = importance_similarity.astype(jnp.bfloat16)
    subtotal_penalty = jnp.sum(example_importance[:, None] * (jax.nn.softplus(couple_odds) - matching_indicator * couple_odds))
    single_number_parts = jnp.stack([subtotal_penalty, odds_sharpness * jnp.sum(importance_similarity * couple_similarity), jnp.sum(importance_similarity)])
    picture_derivative = odds_sharpness * jnp.dot(couple_strength, caption_line_group, preferred_element_type=jnp.float32)
    caption_derivative = (odds_sharpness * jnp.dot(couple_strength.T, picture_line_group, preferred_element_type=jnp.float32)).astype(jnp.bfloat16)
    return picture_derivative, caption_derivative, single_number_parts


def reference(images, caption_vectors, sample_weight, natural_odds_factor, bias):
    odds_sharpness = jnp.exp(natural_odds_factor[0])
    line_start_shift = bias[0]
    image_groups = images.reshape(GROUPS, ROWS, D)
    text_groups = caption_vectors.reshape(GROUPS, ROWS, D)
    weight_groups = sample_weight.reshape(GROUPS, ROWS)
    identity = np.arange(GROUPS)
    bit_width = GROUPS.bit_length() - 1
    plan = [(identity, jnp.eye(ROWS, dtype=jnp.float32))]
    for step_index in range(ROUNDS):
        flipped = step_index * (bit_width - 1) // (ROUNDS - 1)
        plan.append((identity ^ (1 << flipped), jnp.float32(0.0)))
    picture_derivative_sum = jnp.zeros((GROUPS, ROWS, D), jnp.float32)
    text_total = jnp.zeros((GROUPS, ROWS, D), jnp.float32)
    scalar_total = jnp.zeros((3,), jnp.float32)
    for partner, matching_indicator in plan:
        def one_group(outcome_threefold):
            return companion_tile(outcome_threefold[0], outcome_threefold[1], outcome_threefold[2], odds_sharpness, line_start_shift, matching_indicator)

        picture_derivative, caption_derivative, single_number_parts = lax.map(one_group, (image_groups, text_groups[partner], weight_groups))
        picture_derivative_sum = picture_derivative_sum + picture_derivative
        text_total = text_total + lax.optimization_barrier(caption_derivative).astype(jnp.float32)[partner]
        scalar_total = scalar_total + jnp.sum(single_number_parts, axis=0)
    pair_count = TOKENS * ROWS * (ROUNDS + 1)
    loss = jnp.reshape(scalar_total[0] / pair_count, (1,))
    grad_scalars = scalar_total[1:] / pair_count
    return (loss, grad_scalars, picture_derivative_sum.reshape(TOKENS, D).astype(jnp.bfloat16), text_total.reshape(TOKENS, D).astype(jnp.bfloat16))
```

```python
import functools

import jax
import jax.numpy as jnp
from jax import lax
from jax.experimental import pallas as pl
from jax.experimental.pallas import tpu as pltpu
from jax.sharding import PartitionSpec as P

ROUNDS = 3
LONG = 20_000_000_000
PAD = 16
VMEM = pl.BlockSpec(memory_space=pltpu.VMEM)
SMEM = pl.BlockSpec(memory_space=pltpu.SMEM)
ANY = pl.BlockSpec(memory_space=pl.ANY)


def exchange(value, batch_mask, rep_mask=0):
    batch, rep = lax.axis_size("batch"), lax.axis_size("rep")
    if rep_mask == 0:
        return lax.ppermute(value, "batch", [(s, s ^ batch_mask) for s in range(batch)])
    if batch_mask == 0:
        return lax.ppermute(value, "rep", [(s, s ^ rep_mask) for s in range(rep)])
    mask = batch_mask * rep + rep_mask
    return lax.ppermute(value, ("batch", "rep"), [(s, s ^ mask) for s in range(batch * rep)])


def pack_kernel(image_ref, weight_ref, *refs):
    out_ref = refs[-1]
    rows, width = image_ref.shape
    out_ref[:rows, :] = image_ref[...]
    place = lax.broadcasted_iota(jnp.int32, (PAD, rows), 0)
    rest, tail = weight_ref[...], jnp.zeros((PAD, rows), jnp.float32)
    for index in range(3):
        part = rest.astype(jnp.bfloat16).astype(jnp.float32)
        rest = rest - part
        tail = jnp.where(place == index, part, tail)
    out_ref[rows:, :rows] = tail.astype(jnp.bfloat16)
    out_ref[rows:, rows:] = jnp.zeros((PAD, width - rows), jnp.bfloat16)


def pack_weights(images, weight, after=()):
    rows, width = images.shape
    return pl.pallas_call(
        pack_kernel,
        out_shape=jax.ShapeDtypeStruct((rows + PAD, width), images.dtype),
        in_specs=[VMEM, VMEM] + [ANY] * len(after),
        out_specs=VMEM,
        compiler_params=pltpu.CompilerParams(vmem_limit_bytes=4 * 2**20),
    )(images, weight[None], *after)


def pass_kernel(*refs):
    pass


def held_back(value, *after):
    return pl.pallas_call(
        pass_kernel,
        out_shape=jax.ShapeDtypeStruct(value.shape, value.dtype),
        in_specs=[ANY] * (1 + len(after)),
        out_specs=ANY,
        input_output_aliases={0: 0},
        compiler_params=pltpu.CompilerParams(vmem_limit_bytes=2**20),
    )(value, *after)


def add_kernel(count, *refs):
    total = refs[0][...].astype(jnp.float32)
    for ref in refs[1:count]:
        total = total + ref[...].astype(jnp.float32)
    refs[-1][...] = total.astype(refs[-1].dtype)


def add_up(kind, values, after=()):
    return pl.pallas_call(
        functools.partial(add_kernel, len(values)),
        out_shape=jax.ShapeDtypeStruct(values[0].shape, kind),
        in_specs=[VMEM] * len(values) + [ANY] * len(after),
        out_specs=VMEM,
        compiler_params=pltpu.CompilerParams(vmem_limit_bytes=8 * 2**20),
        cost_estimate=pl.CostEstimate(flops=LONG, bytes_accessed=1, transcendentals=0),
    )(*values, *after)


def all_sum_step(value, batch_mask, rep_mask, after=()):
    received = exchange(value, batch_mask, rep_mask)
    beside = add_up(value.dtype, [value], after)
    return add_up(value.dtype, [value, received], (beside,))


def pair_kernel(
    images, texts, after, positive, add_text, add_image, text_types, image_types, *refs
):
    refs = list(refs)
    scalars = refs.pop(0)
    image_refs = [refs.pop(0) for _ in range(images)]
    text_refs = [refs.pop(0) for _ in range(texts)]
    add_text_refs = [refs.pop(0) if flag else None for flag in add_text]
    add_image_refs = [refs.pop(0) if flag else None for flag in add_image]
    del refs[:after]
    text_outs = [refs.pop(0) for _ in range(texts)]
    image_outs = [refs.pop(0) for _ in range(images)]
    sums_out = refs.pop(0)
    coupling = refs.pop(0)
    rows = text_refs[0].shape[0]
    scale, bias = scalars[0], scalars[1]
    totals = [jnp.zeros((1, rows), jnp.float32) for _ in range(3)]
    for i, image_ref in enumerate(image_refs):
        tail = image_ref[rows : rows + PAD, :rows].astype(jnp.float32)
        weight = tail[0:1] + tail[1:2] + tail[2:3]
        for j, text_ref in enumerate(text_refs):
            scores = lax.dot_general(
                text_ref[...],
                image_ref[:rows, :],
                (((1,), (1,)), ((), ())),
                preferred_element_type=jnp.float32,
            )
            logits = scale * scores + bias
            small = jnp.exp(-jnp.abs(logits))
            inverse = 1.0 / (1.0 + small)
            chance = jnp.where(logits >= 0, inverse, small * inverse)
            penalty = jnp.maximum(logits, 0.0) + jnp.log1p(small)
            if positive and i == 0 and j == 0:
                same = lax.broadcasted_iota(jnp.int32, scores.shape, 0) == lax.broadcasted_iota(
                    jnp.int32, scores.shape, 1
                )
                chance = chance - jnp.where(same, 1.0, 0.0)
                penalty = penalty - jnp.where(same, logits, 0.0)
            for k, term in enumerate((penalty, chance * scores, chance)):
                totals[k] = totals[k] + weight * jnp.sum(term, axis=0, keepdims=True)
            coupling[i, j] = (weight * chance).astype(jnp.bfloat16)
    totals[1] = totals[1] * scale
    half = rows // 2
    folded = [total[:, :half] + total[:, half:] for total in totals]
    sums_out[...] = jnp.concatenate(folded + [jnp.zeros((8 - len(folded), half), jnp.float32)])
    for j in range(texts):
        value = None
        for i in range(images):
            term = jnp.dot(
                coupling[i, j], image_refs[i][:rows, :], preferred_element_type=jnp.float32
            )
            value = term if value is None else value + term
        value = value * scale
        if add_text_refs[j] is not None:
            value = value + add_text_refs[j][...].astype(jnp.float32)
        text_outs[j][...] = value.astype(text_types[j])
    for i in range(images):
        value = None
        for j in range(texts):
            term = lax.dot_general(
                coupling[i, j],
                text_refs[j][...],
                (((0,), (0,)), ((), ())),
                preferred_element_type=jnp.float32,
            )
            value = term if value is None else value + term
        value = value * scale
        if add_image_refs[i] is not None:
            value = value + add_image_refs[i][...].astype(jnp.float32)
        image_outs[i][...] = value.astype(image_types[i])


def pair_terms(
    scalars,
    images,
    texts,
    text_types,
    image_types,
    add_text=None,
    add_image=None,
    positive=False,
    after=(),
):
    add_text = add_text or [None] * len(texts)
    add_image = add_image or [None] * len(images)
    rows, width = texts[0].shape
    shape = (rows, width)
    blocks = len(images) * len(texts)
    extra = [value for value in list(add_text) + list(add_image) if value is not None]
    outs = pl.pallas_call(
        functools.partial(
            pair_kernel,
            len(images),
            len(texts),
            len(after),
            positive,
            [value is not None for value in add_text],
            [value is not None for value in add_image],
            text_types,
            image_types,
        ),
        out_shape=[jax.ShapeDtypeStruct(shape, kind) for kind in list(text_types) + list(image_types)]
        + [jax.ShapeDtypeStruct((8, rows // 2), jnp.float32)],
        in_specs=[SMEM]
        + [VMEM] * (len(images) + len(texts) + len(extra))
        + [ANY] * len(after),
        out_specs=[VMEM] * (len(images) + len(texts) + 1),
        scratch_shapes=[pltpu.VMEM((len(images), len(texts), rows, rows), jnp.bfloat16)],
        compiler_params=pltpu.CompilerParams(vmem_limit_bytes=16 * 2**20),
        cost_estimate=pl.CostEstimate(
            flops=LONG,
            bytes_accessed=2 * rows * width * 2 * (len(images) + len(texts)),
            transcendentals=3 * blocks * rows * rows,
        ),
    )(scalars, *images, *texts, *extra, *after)
    return outs[: len(texts)], outs[len(texts) : len(texts) + len(images)], outs[-1]


def add_to(kind, *values):
    total = values[0].astype(jnp.float32)
    for value in values[1:]:
        total = total + value.astype(jnp.float32)
    return total.astype(kind)


def on_device(images, caption_vectors, sample_weight, natural_odds_factor, bias):
    f32, bf16 = jnp.float32, jnp.bfloat16
    groups, rep_count = lax.axis_size("batch"), lax.axis_size("rep")
    rows = images.shape[0]
    bits = groups.bit_length() - 1
    x_bit, z_bit, y_bit = [1 << (step * (bits - 1) // (ROUNDS - 1)) for step in range(ROUNDS)]
    core, far = 1, rep_count // 2
    barrier = lax.optimization_barrier

    scalars = jnp.concatenate([jnp.exp(natural_odds_factor), bias])
    texts = caption_vectors

    texts_z = exchange(texts, z_bit)
    texts_x = exchange(texts, x_bit)
    texts_y = exchange(texts, y_bit)
    own = pack_weights(images, sample_weight)
    own_other = exchange(own, 0, core)
    away = exchange(own, z_bit, far)

    texts_z_x = exchange(texts_z, x_bit)
    texts_z_y = exchange(texts_z, y_bit)
    (near_d0, near_dz, dx, dy), (image_own, image_other), sums_a = pair_terms(
        scalars,
        [own, own_other],
        [texts, texts_z, texts_x, texts_y],
        [f32, f32, bf16, bf16],
        [f32, bf16],
        positive=True,
    )
    image_back = exchange(image_other, 0, core)

    away = held_back(away, sums_a)
    away_other = exchange(away, 0, core)
    (d0, near_dz), (far_part,), sums_b = pair_terms(
        scalars, [away], [texts, texts_z], [f32, f32], [f32], add_text=[near_d0, near_dz]
    )
    (d0, near_dz), (far_other_part,), sums_c = pair_terms(
        scalars, [away_other], [texts, texts_z], [f32, f32], [f32], add_text=[d0, near_dz]
    )
    image_near = add_up(f32, [image_own, image_back], (sums_c,))
    (dzx, dzy), (far_other,), sums_d = pair_terms(
        scalars,
        [away_other],
        [texts_z_x, texts_z_y],
        [f32, f32],
        [bf16],
        add_image=[far_other_part],
        after=(image_near,),
    )
    far_back = exchange(far_other, 0, core)
    (dzx, dzy), (far_own,), sums_e = pair_terms(
        scalars,
        [away],
        [texts_z_x, texts_z_y],
        [bf16, bf16],
        [f32],
        add_text=[dzx, dzy],
        add_image=[far_part],
    )
    dx_back = exchange(held_back(dx, texts_z_x), x_bit)
    dy_back = exchange(held_back(dy, texts_z_y), y_bit)
    dzx_back = exchange(dzx, x_bit)
    dzy_back = exchange(dzy, y_bit)
    away_total = add_up(bf16, [far_own, far_back], (sums_e,))
    image_away = exchange(away_total, z_bit, far)
    d0 = add_up(f32, [d0, dx_back, dy_back])

    sums = add_up(f32, [sums_a, sums_b, sums_c, sums_d, sums_e], (d0, away_total))
    sums = all_sum_step(sums, 0, far)
    sums = all_sum_step(sums, x_bit, 0)
    sums = all_sum_step(sums, z_bit, 0)
    dz_total = add_up(bf16, [near_dz, dzx_back, dzy_back], (sums,))
    dz_back = exchange(dz_total, z_bit)
    sums = all_sum_step(held_back(sums, dz_total), 0, core)
    sums = all_sum_step(sums, 2 * x_bit, 0)
    sums = all_sum_step(sums, 2 * z_bit, 0)
    sums = all_sum_step(sums, y_bit // 2, 0)
    sums = all_sum_step(sums, y_bit, 0)
    totals = jnp.sum(sums, axis=1)

    pair_count = float(rows * rep_count * groups * rows * rep_count * (ROUNDS + 1))
    loss = totals[0:1] / pair_count
    grad_scalars = totals[1:3] / pair_count
    grad_texts = add_up(bf16, [d0, dz_back])
    grad_images = add_up(bf16, [image_near, image_away])
    return loss, grad_scalars, grad_images, grad_texts


def solution(mesh):
    in_specs = (P(("batch", "rep"), None), P(("batch", "rep"), None), P(("batch", "rep")), P(), P())
    out_specs = (P(), P(), P(("batch", "rep"), None), P(("batch", "rep"), None))
    return jax.shard_map(
        on_device, mesh=mesh, in_specs=in_specs, out_specs=out_specs, check_vma=False
    )
```

```python
import functools

import jax
import jax.numpy as jnp
from jax import lax
from jax.experimental import pallas as pl
from jax.experimental.pallas import tpu as pltpu
from jax.sharding import PartitionSpec as P

ROUNDS = 3
LONG = 10_000_000_000
SHORT = 100_000_000
PAD = 16
VMEM = pl.BlockSpec(memory_space=pltpu.VMEM)
SMEM = pl.BlockSpec(memory_space=pltpu.SMEM)
ANY = pl.BlockSpec(memory_space=pl.ANY)
HBM = pl.BlockSpec(memory_space=pltpu.HBM)


def exchange(value, batch_mask, rep_mask=0):
    batch, rep = lax.axis_size("batch"), lax.axis_size("rep")
    if rep_mask == 0:
        return lax.ppermute(value, "batch", [(s, s ^ batch_mask) for s in range(batch)])
    if batch_mask == 0:
        return lax.ppermute(value, "rep", [(s, s ^ rep_mask) for s in range(rep)])
    mask = batch_mask * rep + rep_mask
    return lax.ppermute(value, ("batch", "rep"), [(s, s ^ mask) for s in range(batch * rep)])


def pack_kernel(starts, image_ref, weight_ref, *refs):
    out_refs, held, copied = refs[:-2], refs[-2], refs[-1]
    counts = [out_ref.shape[0] - PAD for out_ref in out_refs]
    copies = [pltpu.make_async_copy(weight_ref, held, copied.at[0])]
    for index, (start, count, out_ref) in enumerate(zip(starts, counts, out_refs)):
        source = image_ref.at[pl.ds(start, count)]
        target = out_ref.at[pl.ds(0, count)]
        copies.append(pltpu.make_async_copy(source, target, copied.at[index + 1]))
    for copy in copies:
        copy.start()
    copies[0].wait()
    for start, count, out_ref in zip(starts, counts, out_refs):
        place = lax.broadcasted_iota(jnp.int32, (PAD, count), 0)
        rest = held[:, start : start + count]
        tail = jnp.zeros((PAD, count), jnp.float32)
        for part_index in range(3):
            part = rest.astype(jnp.bfloat16).astype(jnp.float32)
            rest = rest - part
            tail = jnp.where(place == part_index, part, tail)
        out_ref[count:, :count] = tail.astype(jnp.bfloat16)
        out_ref[count:, count:] = jnp.zeros((PAD, out_ref.shape[1] - count), jnp.bfloat16)
    for copy in copies[1:]:
        copy.wait()


def pack_weights(images, weight, ranges):
    rows, width = images.shape
    return pl.pallas_call(
        functools.partial(pack_kernel, [start for start, _ in ranges]),
        out_shape=[jax.ShapeDtypeStruct((count + PAD, width), images.dtype) for _, count in ranges],
        in_specs=[HBM, HBM],
        out_specs=[VMEM] * len(ranges),
        scratch_shapes=[
            pltpu.VMEM((1, rows), jnp.float32),
            pltpu.SemaphoreType.DMA((len(ranges) + 1,)),
        ],
        cost_estimate=pl.CostEstimate(flops=1, bytes_accessed=1, transcendentals=0),
        compiler_params=pltpu.CompilerParams(vmem_limit_bytes=4 * 2**20),
    )(images, weight[None])


def held_back(value, *after):
    return lax.optimization_barrier((value, *after))[0]


def mark_kernel(*refs):
    refs[-1][...] = jnp.zeros_like(refs[-1])


def beside(*values, flops=LONG):
    return pl.pallas_call(
        mark_kernel,
        out_shape=jax.ShapeDtypeStruct((8, 128), jnp.float32),
        in_specs=[ANY] * len(values),
        out_specs=VMEM,
        compiler_params=pltpu.CompilerParams(vmem_limit_bytes=2**20),
        cost_estimate=pl.CostEstimate(flops=flops, bytes_accessed=1, transcendentals=0),
    )(*values)


def add_kernel(count, pairs, *refs):
    values = [ref[...].astype(jnp.float32) for ref in refs[:count]]
    if pairs:
        values = [values[0] + values[1], values[2] + values[3]]
    total = values[0]
    for value in values[1:]:
        total = total + value
    refs[-1][...] = total.astype(refs[-1].dtype)


def add_up(kind, values, after=(), pairs=False):
    return pl.pallas_call(
        functools.partial(add_kernel, len(values), pairs),
        out_shape=jax.ShapeDtypeStruct(values[0].shape, kind),
        in_specs=[VMEM] * len(values) + [ANY] * len(after),
        out_specs=VMEM,
        compiler_params=pltpu.CompilerParams(vmem_limit_bytes=8 * 2**20),
        cost_estimate=pl.CostEstimate(flops=1, bytes_accessed=1, transcendentals=0),
    )(*values, *after)


def all_sum_step(value, batch_mask, rep_mask, after=()):
    received = exchange(value, batch_mask, rep_mask)
    return add_up(value.dtype, [value, received], (beside(value, *after, flops=SHORT),))


def score_block(scores, weight, scale, bias, positive):
    logits = scale * scores + bias
    small = jnp.exp(-jnp.abs(logits))
    total = 1.0 + small
    inverse = 1.0 / total
    chance = jnp.where(logits >= 0, inverse, small * inverse)
    lost = (small - (total - 1.0)) * inverse
    penalty = jnp.maximum(logits, 0.0) + (jnp.log(total) + lost)
    if positive:
        rows = lax.broadcasted_iota(jnp.int32, scores.shape, 0)
        same = rows == lax.broadcasted_iota(jnp.int32, scores.shape, 1)
        chance = chance - jnp.where(same, 1.0, 0.0)
        penalty = penalty - jnp.where(same, logits, 0.0)
    terms = (penalty, chance * scores, chance)
    sums = [jnp.sum(term, axis=0, keepdims=True) for term in terms]
    return (weight * chance).astype(jnp.bfloat16), [weight * value for value in sums]


def store_sums(sums_out, totals, scale):
    half = totals[0].shape[1] // 2
    totals = [totals[0], totals[1] * scale, totals[2]]
    folded = [total[:, :half] + total[:, half:] for total in totals]
    sums_out[...] = jnp.concatenate(folded + [jnp.zeros((8 - len(folded), half), jnp.float32)])


def pair_kernel(
    image_pieces, text_pieces, after, positive, add_text, add_image, text_types, image_types, *refs
):
    refs = list(refs)
    take = lambda counts: [[refs.pop(0) for _ in range(count)] for count in counts]
    images, texts = len(image_pieces), len(text_pieces)
    scalars = refs.pop(0)
    image_refs, text_refs = take(image_pieces), take(text_pieces)
    add_text_refs = take(add_text)
    add_image_refs = take(add_image)
    del refs[:after]
    text_outs = [refs.pop(0) for _ in range(texts)]
    image_outs = take([len(kinds) for kinds in image_types])
    sums_out, coupling, held = refs
    rows = coupling.shape[-1]
    scale, bias = scalars[0], scalars[1]
    totals = [jnp.zeros((1, rows), jnp.float32) for _ in range(3)]

    slot, image_blocks, text_blocks, weights = 0, [], [], []
    for pieces in text_refs:
        if len(pieces) == 1:
            text_blocks.append(pieces[0])
            continue
        start = 0
        for piece in pieces:
            held[slot, start : start + piece.shape[0]] = piece[...]
            start += piece.shape[0]
        text_blocks.append(held.at[slot])
        slot += 1
    for pieces in image_refs:
        start, parts = 0, []
        for piece in pieces:
            count = piece.shape[0] - PAD
            held[slot, start : start + count] = piece[:count]
            tail = piece[count:, :count].astype(jnp.float32)
            parts.append(tail[0:1] + tail[1:2] + tail[2:3])
            start += count
        image_blocks.append(held.at[slot])
        weights.append(parts[0] if len(parts) == 1 else jnp.concatenate(parts, axis=1))
        slot += 1

    for i, image_ref in enumerate(image_blocks):
        weight = weights[i]
        for j, text_ref in enumerate(text_blocks):
            scores = lax.dot_general(
                text_ref[...],
                image_ref[...],
                (((1,), (1,)), ((), ())),
                preferred_element_type=jnp.float32,
            )
            coupling[i, j], sums = score_block(
                scores, weight, scale, bias, positive and i == 0 and j == 0
            )
            totals = [total + value for total, value in zip(totals, sums)]
    store_sums(sums_out, totals, scale)
    for i in range(images):
        value = None
        for j in range(texts):
            term = lax.dot_general(
                coupling[i, j],
                text_blocks[j][...],
                (((0,), (0,)), ((), ())),
                preferred_element_type=jnp.float32,
            )
            value = term if value is None else value + term
        value = value * scale
        for ref in add_image_refs[i]:
            value = value + ref[...].astype(jnp.float32)
        image_outs[i][0][...] = value.astype(image_types[i][0])
    for j in range(texts):
        value = None
        for i in range(images):
            term = jnp.dot(
                coupling[i, j], image_blocks[i][...], preferred_element_type=jnp.float32
            )
            value = term if value is None else value + term
        value = value * scale
        for ref in add_text_refs[j]:
            value = value + ref[...].astype(jnp.float32)
        text_outs[j][...] = value.astype(text_types[j])


def pair_terms(
    scalars,
    images,
    texts,
    text_types,
    image_types,
    add_text=None,
    add_image=None,
    positive=False,
    after=(),
    flops=1,
):
    add_text = add_text or [[]] * len(texts)
    add_image = add_image or [[]] * len(images)
    rows, width = sum(piece.shape[0] for piece in texts[0]), texts[0][0].shape[1]
    blocks = len(images) * len(texts)
    operands = [piece for pieces in list(images) + list(texts) for piece in pieces]
    operands += [value for values in add_text for value in values]
    operands += [value for values in add_image for value in values]
    image_shapes = [
        jax.ShapeDtypeStruct((rows // len(kinds), width), kind) for kinds in image_types for kind in kinds
    ]
    held = len(images) + sum(len(pieces) > 1 for pieces in texts)
    outs = pl.pallas_call(
        functools.partial(
            pair_kernel,
            [len(pieces) for pieces in images],
            [len(pieces) for pieces in texts],
            len(after),
            positive,
            [len(values) for values in add_text],
            [len(values) for values in add_image],
            text_types,
            image_types,
        ),
        out_shape=[jax.ShapeDtypeStruct((rows, width), kind) for kind in text_types]
        + image_shapes
        + [jax.ShapeDtypeStruct((8, rows // 2), jnp.float32)],
        in_specs=[SMEM] + [VMEM] * len(operands) + [ANY] * len(after),
        out_specs=[VMEM] * (len(texts) + len(image_shapes) + 1),
        scratch_shapes=[
            pltpu.VMEM((len(images), len(texts), rows, rows), jnp.bfloat16),
            pltpu.VMEM((held, rows, width), jnp.bfloat16),
        ],
        compiler_params=pltpu.CompilerParams(vmem_limit_bytes=16 * 2**20),
        cost_estimate=pl.CostEstimate(
            flops=flops, bytes_accessed=1, transcendentals=0
        ),
    )(scalars, *operands, *after)
    image_outs, place = [], len(texts)
    for kinds in image_types:
        image_outs.append(outs[place : place + len(kinds)])
        place += len(kinds)
    return outs[: len(texts)], image_outs, outs[-1]


def on_device(images, caption_vectors, sample_weight, natural_odds_factor, bias):
    f32, bf16 = jnp.float32, jnp.bfloat16
    groups, rep_count = lax.axis_size("batch"), lax.axis_size("rep")
    rows = images.shape[0]
    bits = groups.bit_length() - 1
    x_bit, z_bit, y_bit = [1 << (step * (bits - 1) // (ROUNDS - 1)) for step in range(ROUNDS)]
    core, far = 1, rep_count // 2
    barrier = lax.optimization_barrier

    scalars = jnp.concatenate([jnp.exp(natural_odds_factor), bias])
    texts = caption_vectors
    texts_z = exchange(texts, z_bit)
    texts_x = exchange(texts, x_bit)
    texts_y = exchange(texts, y_bit)
    (own,) = pack_weights(images, sample_weight, [(0, rows)])
    other = exchange(own, 0, core)

    away = exchange(held_back(own, texts_z), z_bit, far)
    texts_zx = exchange(texts_z, x_bit)
    texts_zy = exchange(texts_z, y_bit)
    (d0, dz, dx, dy), ((image_own,), (image_other,)), sums_a = pair_terms(
        scalars,
        [[own], [other]],
        [[texts], [texts_z], [texts_x], [texts_y]],
        [f32, f32, bf16, bf16],
        [[bf16], [bf16]],
        positive=True,
    )
    image_back = exchange(image_other, 0, core)
    image_near = add_up(bf16, [image_own, image_back])

    away = held_back(away, image_near, texts_zx, texts_zy)
    away_other = exchange(away, 0, core)
    dx_back = exchange(held_back(dx, texts_zx), x_bit)
    dy_back = exchange(held_back(dy, texts_zy), y_bit)
    (dzx, dzy), (far_own,), sums_b = pair_terms(
        scalars,
        [[away]],
        [[texts_zx], [texts_zy]],
        [f32, f32],
        [[f32]],
        flops=LONG,
    )
    (d0, dz, dzx, dzy), ((far_other,),), sums_c = pair_terms(
        scalars,
        [[away_other]],
        [[texts], [texts_z], [texts_zx], [texts_zy]],
        [f32, f32, bf16, bf16],
        [[bf16]],
        add_text=[[d0], [dz], [dzx], [dzy]],
        after=(sums_b,),
    )
    near_back = exchange(far_other, 0, core)
    dzx_back = exchange(dzx, x_bit)
    dzy_back = exchange(dzy, y_bit)
    (d0, dz), ((far_total,),), sums_d = pair_terms(
        scalars,
        [[away]],
        [[texts], [texts_z]],
        [bf16, f32],
        [[bf16]],
        add_text=[[d0, dx_back, dy_back], [dz]],
        add_image=[[*far_own, near_back]],
        after=(sums_c,),
    )
    image_away = exchange(far_total, z_bit, far)

    sums = add_up(f32, [sums_a, sums_b, sums_c, sums_d])
    sums = all_sum_step(sums, z_bit, 0)
    sums = all_sum_step(sums, 0, far)
    dz_total = add_up(bf16, [dz, dzx_back, dzy_back], (sums,))
    dz_back = exchange(dz_total, z_bit)
    sums = all_sum_step(held_back(sums, dz_total), 0, core)
    sums = all_sum_step(sums, 3 * x_bit, 0)
    sums = all_sum_step(sums, 2 * x_bit, 0)
    sums = all_sum_step(sums, y_bit // 2, 0)
    sums = all_sum_step(sums, y_bit // 2 * 3, 0)
    received = exchange(sums, 2 * z_bit)
    grad_images = (image_near.astype(f32) + image_away).astype(bf16)
    sums = add_up(f32, [sums, received], (grad_images,))
    totals = jnp.sum(sums, axis=1)

    pair_count = float(rows * rep_count * groups * rows * rep_count * (ROUNDS + 1))
    loss = totals[0:1] / pair_count
    grad_scalars = totals[1:3] / pair_count
    grad_texts = (d0.astype(f32) + dz_back).astype(bf16)
    return loss, grad_scalars, grad_images, grad_texts


def solution(mesh):
    in_specs = (P(("batch", "rep"), None), P(("batch", "rep"), None), P(("batch", "rep")), P(), P())
    out_specs = (P(), P(), P(("batch", "rep"), None), P(("batch", "rep"), None))
    return jax.shard_map(
        on_device, mesh=mesh, in_specs=in_specs, out_specs=out_specs, check_vma=False
    )
```

```python
import functools

import jax
import jax.numpy as jnp
from jax import lax
from jax.experimental import pallas as pl
from jax.experimental.pallas import tpu as pltpu
from jax.sharding import PartitionSpec as P

ROUNDS = 3
LONG = 10_000_000_000
SHORT = 100_000_000
PAD = 16
VMEM = pl.BlockSpec(memory_space=pltpu.VMEM)
SMEM = pl.BlockSpec(memory_space=pltpu.SMEM)
ANY = pl.BlockSpec(memory_space=pl.ANY)
HBM = pl.BlockSpec(memory_space=pltpu.HBM)


def exchange(value, batch_mask, rep_mask=0):
    batch, rep = lax.axis_size("batch"), lax.axis_size("rep")
    if rep_mask == 0:
        return lax.ppermute(value, "batch", [(s, s ^ batch_mask) for s in range(batch)])
    if batch_mask == 0:
        return lax.ppermute(value, "rep", [(s, s ^ rep_mask) for s in range(rep)])
    mask = batch_mask * rep + rep_mask
    return lax.ppermute(value, ("batch", "rep"), [(s, s ^ mask) for s in range(batch * rep)])


def pack_kernel(starts, image_ref, weight_ref, *refs):
    out_refs, held, copied = refs[:-2], refs[-2], refs[-1]
    counts = [out_ref.shape[0] - PAD for out_ref in out_refs]
    copies = [pltpu.make_async_copy(weight_ref, held, copied.at[0])]
    for index, (start, count, out_ref) in enumerate(zip(starts, counts, out_refs)):
        source = image_ref.at[pl.ds(start, count)]
        target = out_ref.at[pl.ds(0, count)]
        copies.append(pltpu.make_async_copy(source, target, copied.at[index + 1]))
    for copy in copies:
        copy.start()
    copies[0].wait()
    for start, count, out_ref in zip(starts, counts, out_refs):
        place = lax.broadcasted_iota(jnp.int32, (PAD, count), 0)
        rest = held[:, start : start + count]
        tail = jnp.zeros((PAD, count), jnp.float32)
        for part_index in range(3):
            part = rest.astype(jnp.bfloat16).astype(jnp.float32)
            rest = rest - part
            tail = jnp.where(place == part_index, part, tail)
        out_ref[count:, :count] = tail.astype(jnp.bfloat16)
        out_ref[count:, count:] = jnp.zeros((PAD, out_ref.shape[1] - count), jnp.bfloat16)
    for copy in copies[1:]:
        copy.wait()


def pack_weights(images, weight, ranges):
    rows, width = images.shape
    return pl.pallas_call(
        functools.partial(pack_kernel, [start for start, _ in ranges]),
        out_shape=[jax.ShapeDtypeStruct((count + PAD, width), images.dtype) for _, count in ranges],
        in_specs=[HBM, HBM],
        out_specs=[VMEM] * len(ranges),
        scratch_shapes=[
            pltpu.VMEM((1, rows), jnp.float32),
            pltpu.SemaphoreType.DMA((len(ranges) + 1,)),
        ],
        cost_estimate=pl.CostEstimate(flops=1, bytes_accessed=1, transcendentals=0),
        compiler_params=pltpu.CompilerParams(vmem_limit_bytes=4 * 2**20),
    )(images, weight[None])


def held_back(value, *after):
    return lax.optimization_barrier((value, *after))[0]


def mark_kernel(*refs):
    refs[-1][...] = jnp.zeros_like(refs[-1])


def beside(*values, flops=LONG):
    return pl.pallas_call(
        mark_kernel,
        out_shape=jax.ShapeDtypeStruct((8, 128), jnp.float32),
        in_specs=[ANY] * len(values),
        out_specs=VMEM,
        compiler_params=pltpu.CompilerParams(vmem_limit_bytes=2**20),
        cost_estimate=pl.CostEstimate(flops=flops, bytes_accessed=1, transcendentals=0),
    )(*values)


def add_kernel(count, pairs, *refs):
    values = [ref[...].astype(jnp.float32) for ref in refs[:count]]
    if pairs:
        values = [values[0] + values[1], values[2] + values[3]]
    total = values[0]
    for value in values[1:]:
        total = total + value
    refs[-1][...] = total.astype(refs[-1].dtype)


def add_up(kind, values, after=(), pairs=False):
    return pl.pallas_call(
        functools.partial(add_kernel, len(values), pairs),
        out_shape=jax.ShapeDtypeStruct(values[0].shape, kind),
        in_specs=[VMEM] * len(values) + [ANY] * len(after),
        out_specs=VMEM,
        compiler_params=pltpu.CompilerParams(vmem_limit_bytes=8 * 2**20),
        cost_estimate=pl.CostEstimate(flops=1, bytes_accessed=1, transcendentals=0),
    )(*values, *after)


def all_sum_step(value, batch_mask, rep_mask, after=()):
    received = exchange(value, batch_mask, rep_mask)
    return add_up(value.dtype, [value, received], (beside(value, *after, flops=SHORT),))


def score_block(scores, weight, scale, bias, positive):
    logits = scale * scores + bias
    small = jnp.exp(-jnp.abs(logits))
    total = 1.0 + small
    inverse = 1.0 / total
    chance = jnp.where(logits >= 0, inverse, small * inverse)
    lost = (small - (total - 1.0)) * inverse
    penalty = jnp.maximum(logits, 0.0) + (jnp.log(total) + lost)
    if positive:
        rows = lax.broadcasted_iota(jnp.int32, scores.shape, 0)
        same = rows == lax.broadcasted_iota(jnp.int32, scores.shape, 1)
        chance = chance - jnp.where(same, 1.0, 0.0)
        penalty = penalty - jnp.where(same, logits, 0.0)
    terms = (penalty, chance * scores, chance)
    sums = [jnp.sum(term, axis=0, keepdims=True) for term in terms]
    return (weight * chance).astype(jnp.bfloat16), [weight * value for value in sums]


def store_sums(sums_out, totals, scale):
    half = totals[0].shape[1] // 2
    totals = [totals[0], totals[1] * scale, totals[2]]
    folded = [total[:, :half] + total[:, half:] for total in totals]
    sums_out[...] = jnp.concatenate(folded + [jnp.zeros((8 - len(folded), half), jnp.float32)])


def pair_kernel(
    image_pieces, text_pieces, after, positive, add_text, add_image, text_types, image_types, *refs
):
    refs = list(refs)
    take = lambda counts: [[refs.pop(0) for _ in range(count)] for count in counts]
    images, texts = len(image_pieces), len(text_pieces)
    scalars = refs.pop(0)
    image_refs, text_refs = take(image_pieces), take(text_pieces)
    add_text_refs = take(add_text)
    add_image_refs = take(add_image)
    del refs[:after]
    text_outs = [refs.pop(0) for _ in range(texts)]
    image_outs = take([len(kinds) for kinds in image_types])
    sums_out, coupling, held = refs
    rows = coupling.shape[-1]
    scale, bias = scalars[0], scalars[1]
    totals = [jnp.zeros((1, rows), jnp.float32) for _ in range(3)]

    slot, image_blocks, text_blocks, weights = 0, [], [], []
    for pieces in text_refs:
        if len(pieces) == 1:
            text_blocks.append(pieces[0])
            continue
        start = 0
        for piece in pieces:
            held[slot, start : start + piece.shape[0]] = piece[...]
            start += piece.shape[0]
        text_blocks.append(held.at[slot])
        slot += 1
    for pieces in image_refs:
        start, parts = 0, []
        for piece in pieces:
            count = piece.shape[0] - PAD
            held[slot, start : start + count] = piece[:count]
            tail = piece[count:, :count].astype(jnp.float32)
            parts.append(tail[0:1] + tail[1:2] + tail[2:3])
            start += count
        image_blocks.append(held.at[slot])
        weights.append(parts[0] if len(parts) == 1 else jnp.concatenate(parts, axis=1))
        slot += 1

    for i, image_ref in enumerate(image_blocks):
        weight = weights[i]
        for j, text_ref in enumerate(text_blocks):
            scores = lax.dot_general(
                text_ref[...],
                image_ref[...],
                (((1,), (1,)), ((), ())),
                preferred_element_type=jnp.float32,
            )
            coupling[i, j], sums = score_block(
                scores, weight, scale, bias, positive and i == 0 and j == 0
            )
            totals = [total + value for total, value in zip(totals, sums)]
    store_sums(sums_out, totals, scale)
    for i in range(images):
        value = None
        for j in range(texts):
            term = lax.dot_general(
                coupling[i, j],
                text_blocks[j][...],
                (((0,), (0,)), ((), ())),
                preferred_element_type=jnp.float32,
            )
            value = term if value is None else value + term
        value = value * scale
        for ref in add_image_refs[i]:
            value = value + ref[...].astype(jnp.float32)
        image_outs[i][0][...] = value.astype(image_types[i][0])
    for j in range(texts):
        value = None
        for i in range(images):
            term = jnp.dot(
                coupling[i, j], image_blocks[i][...], preferred_element_type=jnp.float32
            )
            value = term if value is None else value + term
        value = value * scale
        for ref in add_text_refs[j]:
            value = value + ref[...].astype(jnp.float32)
        text_outs[j][...] = value.astype(text_types[j])


def pair_terms(
    scalars,
    images,
    texts,
    text_types,
    image_types,
    add_text=None,
    add_image=None,
    positive=False,
    after=(),
    flops=1,
):
    add_text = add_text or [[]] * len(texts)
    add_image = add_image or [[]] * len(images)
    rows, width = sum(piece.shape[0] for piece in texts[0]), texts[0][0].shape[1]
    blocks = len(images) * len(texts)
    operands = [piece for pieces in list(images) + list(texts) for piece in pieces]
    operands += [value for values in add_text for value in values]
    operands += [value for values in add_image for value in values]
    image_shapes = [
        jax.ShapeDtypeStruct((rows // len(kinds), width), kind) for kinds in image_types for kind in kinds
    ]
    held = len(images) + sum(len(pieces) > 1 for pieces in texts)
    outs = pl.pallas_call(
        functools.partial(
            pair_kernel,
            [len(pieces) for pieces in images],
            [len(pieces) for pieces in texts],
            len(after),
            positive,
            [len(values) for values in add_text],
            [len(values) for values in add_image],
            text_types,
            image_types,
        ),
        out_shape=[jax.ShapeDtypeStruct((rows, width), kind) for kind in text_types]
        + image_shapes
        + [jax.ShapeDtypeStruct((8, rows // 2), jnp.float32)],
        in_specs=[SMEM] + [VMEM] * len(operands) + [ANY] * len(after),
        out_specs=[VMEM] * (len(texts) + len(image_shapes) + 1),
        scratch_shapes=[
            pltpu.VMEM((len(images), len(texts), rows, rows), jnp.bfloat16),
            pltpu.VMEM((held, rows, width), jnp.bfloat16),
        ],
        compiler_params=pltpu.CompilerParams(vmem_limit_bytes=16 * 2**20),
        cost_estimate=pl.CostEstimate(
            flops=flops, bytes_accessed=1, transcendentals=0
        ),
    )(scalars, *operands, *after)
    image_outs, place = [], len(texts)
    for kinds in image_types:
        image_outs.append(outs[place : place + len(kinds)])
        place += len(kinds)
    return outs[: len(texts)], image_outs, outs[-1]


def on_device(images, caption_vectors, sample_weight, natural_odds_factor, bias):
    f32, bf16 = jnp.float32, jnp.bfloat16
    groups, rep_count = lax.axis_size("batch"), lax.axis_size("rep")
    rows = images.shape[0]
    bits = groups.bit_length() - 1
    x_bit, z_bit, y_bit = [1 << (step * (bits - 1) // (ROUNDS - 1)) for step in range(ROUNDS)]
    core, far = 1, rep_count // 2
    barrier = lax.optimization_barrier

    scalars = jnp.concatenate([jnp.exp(natural_odds_factor), bias])
    texts = caption_vectors
    cut = rows // 4
    texts_z0 = exchange(texts[:cut], z_bit)
    texts_z1 = exchange(texts[cut:], z_bit)
    texts_z = jnp.concatenate([texts_z0, texts_z1])
    texts_x = exchange(texts, x_bit)
    texts_y = exchange(texts, y_bit)
    (own,) = pack_weights(images, sample_weight, [(0, rows)])
    other = exchange(own, 0, core)

    (d0,), ((image_own,), (image_other,)), sums_a = pair_terms(
        scalars, [[own], [other]], [[texts]], [f32], [[f32], [f32]], positive=True
    )
    away = exchange(held_back(own, texts_z0), z_bit, far)
    texts_zx = exchange(texts_z, x_bit)
    texts_zy = exchange(texts_z, y_bit)
    (dz, dx, dy), ((image_own,), (image_other,)), sums_b = pair_terms(
        scalars,
        [[own], [other]],
        [[texts_z], [texts_x], [texts_y]],
        [f32, bf16, bf16],
        [[bf16], [bf16]],
        add_image=[[image_own], [image_other]],
        after=(sums_a,),
    )
    image_back = exchange(image_other, 0, core)

    away = held_back(away, sums_b)
    away_other = exchange(away, 0, core)
    (d0, dz), (far_own,), sums_c = pair_terms(
        scalars,
        [[away]],
        [[texts], [texts_z]],
        [f32, f32],
        [[f32]],
        add_text=[[d0], [dz]],
        flops=LONG,
    )
    (d0, dz), (far_other,), sums_d = pair_terms(
        scalars,
        [[away_other]],
        [[texts], [texts_z]],
        [bf16, f32],
        [[f32]],
        add_text=[[d0], [dz]],
        after=(sums_c,),
    )
    (dzx, dzy), ((far_own,), (far_other,)), sums_e = pair_terms(
        scalars,
        [[away], [away_other]],
        [[texts_zx], [texts_zy]],
        [bf16, bf16],
        [[f32], [bf16]],
        add_image=[far_own, far_other],
        after=(sums_d,),
    )
    near_back = exchange(far_other, 0, core)
    dzx_back = exchange(dzx, x_bit)
    dzy_back = exchange(dzy, y_bit)
    far_total = add_up(bf16, [far_own, near_back], (beside(sums_e),))
    image_away = exchange(far_total, z_bit, far)
    image_near = add_up(bf16, [image_own, image_back], (far_total,))

    sums = add_up(f32, [sums_a, sums_b, sums_c, sums_d, sums_e], (far_total, image_near))
    sums = all_sum_step(sums, z_bit, 0)
    sums = all_sum_step(sums, 0, far)
    dz_total = add_up(bf16, [dz, dzx_back, dzy_back], (sums,))
    dz_back = exchange(dz_total, z_bit)
    dx_back = exchange(held_back(dx, far_total), x_bit)
    dy_back = exchange(held_back(dy, far_total), y_bit)
    sums = all_sum_step(held_back(sums, dz_total), 0, core)
    sums = all_sum_step(sums, 3 * x_bit, 0)
    sums = all_sum_step(sums, 2 * x_bit, 0)
    sums = all_sum_step(sums, y_bit // 2, 0)
    sums = all_sum_step(sums, y_bit // 2 * 3, 0)
    received = exchange(sums, 2 * z_bit)
    d0 = add_up(bf16, [d0, dx_back, dy_back])
    grad_images = (image_near.astype(f32) + image_away).astype(bf16)
    sums = add_up(f32, [sums, received], (grad_images, d0))
    totals = jnp.sum(sums, axis=1)

    pair_count = float(rows * rep_count * groups * rows * rep_count * (ROUNDS + 1))
    loss = totals[0:1] / pair_count
    grad_scalars = totals[1:3] / pair_count
    grad_texts = (d0.astype(f32) + dz_back).astype(bf16)
    return loss, grad_scalars, grad_images, grad_texts


def solution(mesh):
    in_specs = (P(("batch", "rep"), None), P(("batch", "rep"), None), P(("batch", "rep")), P(), P())
    out_specs = (P(), P(), P(("batch", "rep"), None), P(("batch", "rep"), None))
    return jax.shard_map(
        on_device, mesh=mesh, in_specs=in_specs, out_specs=out_specs, check_vma=False
    )
```

```python
import functools

import jax
import jax.numpy as jnp
from jax import lax
from jax.experimental import pallas as pl
from jax.experimental.pallas import tpu as pltpu
from jax.sharding import PartitionSpec as P

ROUNDS = 3
LONG = 10_000_000_000
SHORT = 100_000_000
PAD = 16
VMEM = pl.BlockSpec(memory_space=pltpu.VMEM)
SMEM = pl.BlockSpec(memory_space=pltpu.SMEM)
ANY = pl.BlockSpec(memory_space=pl.ANY)
HBM = pl.BlockSpec(memory_space=pltpu.HBM)


def exchange(value, batch_mask, rep_mask=0):
    batch, rep = lax.axis_size("batch"), lax.axis_size("rep")
    if rep_mask == 0:
        return lax.ppermute(value, "batch", [(s, s ^ batch_mask) for s in range(batch)])
    if batch_mask == 0:
        return lax.ppermute(value, "rep", [(s, s ^ rep_mask) for s in range(rep)])
    mask = batch_mask * rep + rep_mask
    return lax.ppermute(value, ("batch", "rep"), [(s, s ^ mask) for s in range(batch * rep)])


def pack_kernel(starts, image_ref, weight_ref, *refs):
    out_refs, held, copied = refs[:-2], refs[-2], refs[-1]
    counts = [out_ref.shape[0] - PAD for out_ref in out_refs]
    copies = [pltpu.make_async_copy(weight_ref, held, copied.at[0])]
    for index, (start, count, out_ref) in enumerate(zip(starts, counts, out_refs)):
        source = image_ref.at[pl.ds(start, count)]
        target = out_ref.at[pl.ds(0, count)]
        copies.append(pltpu.make_async_copy(source, target, copied.at[index + 1]))
    for copy in copies:
        copy.start()
    copies[0].wait()
    for start, count, out_ref in zip(starts, counts, out_refs):
        place = lax.broadcasted_iota(jnp.int32, (PAD, count), 0)
        rest = held[:, start : start + count]
        tail = jnp.zeros((PAD, count), jnp.float32)
        for part_index in range(3):
            part = rest.astype(jnp.bfloat16).astype(jnp.float32)
            rest = rest - part
            tail = jnp.where(place == part_index, part, tail)
        out_ref[count:, :count] = tail.astype(jnp.bfloat16)
        out_ref[count:, count:] = jnp.zeros((PAD, out_ref.shape[1] - count), jnp.bfloat16)
    for copy in copies[1:]:
        copy.wait()


def pack_weights(images, weight, ranges):
    rows, width = images.shape
    return pl.pallas_call(
        functools.partial(pack_kernel, [start for start, _ in ranges]),
        out_shape=[jax.ShapeDtypeStruct((count + PAD, width), images.dtype) for _, count in ranges],
        in_specs=[HBM, HBM],
        out_specs=[VMEM] * len(ranges),
        scratch_shapes=[
            pltpu.VMEM((1, rows), jnp.float32),
            pltpu.SemaphoreType.DMA((len(ranges) + 1,)),
        ],
        cost_estimate=pl.CostEstimate(flops=1, bytes_accessed=1, transcendentals=0),
        compiler_params=pltpu.CompilerParams(vmem_limit_bytes=4 * 2**20),
    )(images, weight[None])


def held_back(value, *after):
    return lax.optimization_barrier((value, *after))[0]


def mark_kernel(*refs):
    refs[-1][...] = jnp.zeros_like(refs[-1])


def beside(*values, flops=LONG):
    return pl.pallas_call(
        mark_kernel,
        out_shape=jax.ShapeDtypeStruct((8, 128), jnp.float32),
        in_specs=[ANY] * len(values),
        out_specs=VMEM,
        compiler_params=pltpu.CompilerParams(vmem_limit_bytes=2**20),
        cost_estimate=pl.CostEstimate(flops=flops, bytes_accessed=1, transcendentals=0),
    )(*values)


def add_kernel(count, pairs, *refs):
    values = [ref[...].astype(jnp.float32) for ref in refs[:count]]
    if pairs:
        values = [values[0] + values[1], values[2] + values[3]]
    total = values[0]
    for value in values[1:]:
        total = total + value
    refs[-1][...] = total.astype(refs[-1].dtype)


def add_up(kind, values, after=(), pairs=False):
    return pl.pallas_call(
        functools.partial(add_kernel, len(values), pairs),
        out_shape=jax.ShapeDtypeStruct(values[0].shape, kind),
        in_specs=[VMEM] * len(values) + [ANY] * len(after),
        out_specs=VMEM,
        compiler_params=pltpu.CompilerParams(vmem_limit_bytes=8 * 2**20),
        cost_estimate=pl.CostEstimate(flops=1, bytes_accessed=1, transcendentals=0),
    )(*values, *after)


def all_sum_step(value, batch_mask, rep_mask, after=()):
    received = exchange(value, batch_mask, rep_mask)
    return add_up(value.dtype, [value, received], (beside(value, *after, flops=SHORT),))


def score_block(scores, weight, scale, bias, positive):
    logits = scale * scores + bias
    small = jnp.exp(-jnp.abs(logits))
    total = 1.0 + small
    inverse = 1.0 / total
    chance = jnp.where(logits >= 0, inverse, small * inverse)
    lost = (small - (total - 1.0)) * inverse
    penalty = jnp.maximum(logits, 0.0) + (jnp.log(total) + lost)
    if positive:
        rows = lax.broadcasted_iota(jnp.int32, scores.shape, 0)
        same = rows == lax.broadcasted_iota(jnp.int32, scores.shape, 1)
        chance = chance - jnp.where(same, 1.0, 0.0)
        penalty = penalty - jnp.where(same, logits, 0.0)
    terms = (penalty, chance * scores, chance)
    sums = [jnp.sum(term, axis=0, keepdims=True) for term in terms]
    return (weight * chance).astype(jnp.bfloat16), [weight * value for value in sums]


def store_sums(sums_out, totals, scale):
    half = totals[0].shape[1] // 2
    totals = [totals[0], totals[1] * scale, totals[2]]
    folded = [total[:, :half] + total[:, half:] for total in totals]
    sums_out[...] = jnp.concatenate(folded + [jnp.zeros((8 - len(folded), half), jnp.float32)])


def pair_kernel(
    image_pieces, text_pieces, after, positive, add_text, add_image, text_types, image_types, *refs
):
    refs = list(refs)
    take = lambda counts: [[refs.pop(0) for _ in range(count)] for count in counts]
    images, texts = len(image_pieces), len(text_pieces)
    scalars = refs.pop(0)
    image_refs, text_refs = take(image_pieces), take(text_pieces)
    add_text_refs = take(add_text)
    add_image_refs = take(add_image)
    del refs[:after]
    text_outs = [refs.pop(0) for _ in range(texts)]
    image_outs = take([len(kinds) for kinds in image_types])
    sums_out, coupling, held = refs
    rows = coupling.shape[-1]
    scale, bias = scalars[0], scalars[1]
    totals = [jnp.zeros((1, rows), jnp.float32) for _ in range(3)]

    slot, image_blocks, text_blocks, weights = 0, [], [], []
    for pieces in text_refs:
        if len(pieces) == 1:
            text_blocks.append(pieces[0])
            continue
        start = 0
        for piece in pieces:
            held[slot, start : start + piece.shape[0]] = piece[...]
            start += piece.shape[0]
        text_blocks.append(held.at[slot])
        slot += 1
    for pieces in image_refs:
        start, parts = 0, []
        for piece in pieces:
            count = piece.shape[0] - PAD
            held[slot, start : start + count] = piece[:count]
            tail = piece[count:, :count].astype(jnp.float32)
            parts.append(tail[0:1] + tail[1:2] + tail[2:3])
            start += count
        image_blocks.append(held.at[slot])
        weights.append(parts[0] if len(parts) == 1 else jnp.concatenate(parts, axis=1))
        slot += 1

    for i, image_ref in enumerate(image_blocks):
        weight = weights[i]
        for j, text_ref in enumerate(text_blocks):
            scores = lax.dot_general(
                text_ref[...],
                image_ref[...],
                (((1,), (1,)), ((), ())),
                preferred_element_type=jnp.float32,
            )
            coupling[i, j], sums = score_block(
                scores, weight, scale, bias, positive and i == 0 and j == 0
            )
            totals = [total + value for total, value in zip(totals, sums)]
    store_sums(sums_out, totals, scale)
    for i in range(images):
        value = None
        for j in range(texts):
            term = lax.dot_general(
                coupling[i, j],
                text_blocks[j][...],
                (((0,), (0,)), ((), ())),
                preferred_element_type=jnp.float32,
            )
            value = term if value is None else value + term
        value = value * scale
        for ref in add_image_refs[i]:
            value = value + ref[...].astype(jnp.float32)
        image_outs[i][0][...] = value.astype(image_types[i][0])
    for j in range(texts):
        value = None
        for i in range(images):
            term = jnp.dot(
                coupling[i, j], image_blocks[i][...], preferred_element_type=jnp.float32
            )
            value = term if value is None else value + term
        value = value * scale
        for ref in add_text_refs[j]:
            value = value + ref[...].astype(jnp.float32)
        text_outs[j][...] = value.astype(text_types[j])


def pair_terms(
    scalars,
    images,
    texts,
    text_types,
    image_types,
    add_text=None,
    add_image=None,
    positive=False,
    after=(),
    flops=1,
):
    add_text = add_text or [[]] * len(texts)
    add_image = add_image or [[]] * len(images)
    rows, width = sum(piece.shape[0] for piece in texts[0]), texts[0][0].shape[1]
    blocks = len(images) * len(texts)
    operands = [piece for pieces in list(images) + list(texts) for piece in pieces]
    operands += [value for values in add_text for value in values]
    operands += [value for values in add_image for value in values]
    image_shapes = [
        jax.ShapeDtypeStruct((rows // len(kinds), width), kind) for kinds in image_types for kind in kinds
    ]
    held = len(images) + sum(len(pieces) > 1 for pieces in texts)
    outs = pl.pallas_call(
        functools.partial(
            pair_kernel,
            [len(pieces) for pieces in images],
            [len(pieces) for pieces in texts],
            len(after),
            positive,
            [len(values) for values in add_text],
            [len(values) for values in add_image],
            text_types,
            image_types,
        ),
        out_shape=[jax.ShapeDtypeStruct((rows, width), kind) for kind in text_types]
        + image_shapes
        + [jax.ShapeDtypeStruct((8, rows // 2), jnp.float32)],
        in_specs=[SMEM] + [VMEM] * len(operands) + [ANY] * len(after),
        out_specs=[VMEM] * (len(texts) + len(image_shapes) + 1),
        scratch_shapes=[
            pltpu.VMEM((len(images), len(texts), rows, rows), jnp.bfloat16),
            pltpu.VMEM((held, rows, width), jnp.bfloat16),
        ],
        compiler_params=pltpu.CompilerParams(vmem_limit_bytes=16 * 2**20),
        cost_estimate=pl.CostEstimate(
            flops=flops, bytes_accessed=1, transcendentals=0
        ),
    )(scalars, *operands, *after)
    image_outs, place = [], len(texts)
    for kinds in image_types:
        image_outs.append(outs[place : place + len(kinds)])
        place += len(kinds)
    return outs[: len(texts)], image_outs, outs[-1]


def on_device(images, caption_vectors, sample_weight, natural_odds_factor, bias):
    f32, bf16 = jnp.float32, jnp.bfloat16
    groups, rep_count = lax.axis_size("batch"), lax.axis_size("rep")
    rows = images.shape[0]
    bits = groups.bit_length() - 1
    x_bit, z_bit, y_bit = [1 << (step * (bits - 1) // (ROUNDS - 1)) for step in range(ROUNDS)]
    core, far = 1, rep_count // 2
    barrier = lax.optimization_barrier

    scalars = jnp.concatenate([jnp.exp(natural_odds_factor), bias])
    texts = caption_vectors
    cut = rows // 4
    texts_z0 = exchange(texts[:cut], z_bit)
    texts_z1 = exchange(texts[cut:], z_bit)
    texts_z = jnp.concatenate([texts_z0, texts_z1])
    texts_x = exchange(texts, x_bit)
    texts_y = exchange(texts, y_bit)
    (own,) = pack_weights(images, sample_weight, [(0, rows)])
    other = exchange(own, 0, core)

    (d0,), ((image_own,), (image_other,)), sums_a = pair_terms(
        scalars, [[own], [other]], [[texts]], [f32], [[f32], [f32]], positive=True
    )
    away = exchange(held_back(own, texts_z0), z_bit, far)
    texts_zx = exchange(texts_z, x_bit)
    texts_zy = exchange(texts_z, y_bit)
    (dz, dx, dy), ((image_own,), (image_other,)), sums_b = pair_terms(
        scalars,
        [[own], [other]],
        [[texts_z], [texts_x], [texts_y]],
        [f32, bf16, bf16],
        [[bf16], [bf16]],
        add_image=[[image_own], [image_other]],
        after=(sums_a,),
    )
    image_back = exchange(image_other, 0, core)

    away = held_back(away, sums_b)
    away_other = exchange(away, 0, core)
    (d0, dz), (far_own,), sums_c = pair_terms(
        scalars,
        [[away]],
        [[texts], [texts_z]],
        [f32, f32],
        [[f32]],
        add_text=[[d0], [dz]],
        flops=LONG,
    )
    (d0, dz), (far_other,), sums_d = pair_terms(
        scalars,
        [[away_other]],
        [[texts], [texts_z]],
        [bf16, f32],
        [[f32]],
        add_text=[[d0], [dz]],
        after=(sums_c,),
    )
    (dzx, dzy), ((far_own,), (far_other,)), sums_e = pair_terms(
        scalars,
        [[away], [away_other]],
        [[texts_zx], [texts_zy]],
        [bf16, bf16],
        [[f32], [bf16]],
        add_image=[far_own, far_other],
        after=(sums_d,),
    )
    sums = add_up(f32, [sums_a, sums_b, sums_c, sums_d, sums_e])
    received = exchange(sums, 0, core)
    near_back = exchange(far_other, 0, core)
    dzx_back = exchange(dzx, x_bit)
    dzy_back = exchange(dzy, y_bit)
    mark = beside(sums_e)
    sums = add_up(f32, [sums, received], (mark,))
    far_total = add_up(bf16, [far_own, near_back], (mark, sums))
    image_away = exchange(far_total, z_bit, far)
    image_near = add_up(bf16, [image_own, image_back], (far_total,))

    sums = all_sum_step(held_back(sums, far_total), z_bit, 0)
    sums = all_sum_step(sums, 0, far)
    dz_total = add_up(bf16, [dz, dzx_back, dzy_back], (sums,))
    dz_back = exchange(dz_total, z_bit)
    dx_back = exchange(held_back(dx, far_total), x_bit)
    dy_back = exchange(held_back(dy, far_total), y_bit)
    sums = all_sum_step(held_back(sums, dz_total), 3 * x_bit, 0)
    sums = all_sum_step(sums, 2 * x_bit, 0)
    sums = all_sum_step(sums, y_bit // 2, 0)
    sums = all_sum_step(sums, y_bit // 2 * 3, 0)
    received = exchange(sums, 2 * z_bit)
    d0 = add_up(bf16, [d0, dx_back, dy_back])
    grad_images = (image_near.astype(f32) + image_away).astype(bf16)
    sums = add_up(f32, [sums, received], (grad_images, d0))
    totals = jnp.sum(sums, axis=1)

    pair_count = float(rows * rep_count * groups * rows * rep_count * (ROUNDS + 1))
    loss = totals[0:1] / pair_count
    grad_scalars = totals[1:3] / pair_count
    grad_texts = (d0.astype(f32) + dz_back).astype(bf16)
    return loss, grad_scalars, grad_images, grad_texts


def solution(mesh):
    in_specs = (P(("batch", "rep"), None), P(("batch", "rep"), None), P(("batch", "rep")), P(), P())
    out_specs = (P(), P(), P(("batch", "rep"), None), P(("batch", "rep"), None))
    return jax.shard_map(
        on_device, mesh=mesh, in_specs=in_specs, out_specs=out_specs, check_vma=False
    )
```
